32 devices in a mesh: comp: 4 (over y, x), dom: 8 (over z, core).
Axes of the slice: x: 2, y: 2, z: 4, core: 2. Of those that a mesh axis runs over, the one named last changes fastest.
Arguments:
- model_state: bfloat16 [4, 1024, 48, 128], P('comp', 'dom'), may hold values from -6 to 6
- coefficient: bfloat16 [4, 1024, 48, 128], P('comp', 'dom'), may hold values from 0.049804688 to 0.5
- stencil_blocks: bfloat16 [4, 7, 128, 128], P('comp'), may hold values from -0.1875 to 0.1875
- neighbours: int32 [4, 1024, 7], P('comp', 'dom'), may hold values from 0 to 191
- land_mask: int32 [1024, 128], P('dom'), may hold values 0 or 1
- surface_flux: bfloat16 [4, 1024, 20, 128], P('comp', 'dom'), may hold values from -6 to 6
- remap_pairs: int32 [4, 1024, 2], P('comp', 'dom'), may hold values from 0 to 4095, as said below
- remap_weights: bfloat16 [4, 1024, 2, 128, 128], P('comp', 'dom'), may hold values from -0.5 to 0.5
Outputs:
- next_state: bfloat16 [4, 1024, 48, 128], P('comp', 'dom')
- remapped: bfloat16 [4, 1024, 20, 128], P('comp', 'dom')
The draws below stay inside these ranges and needn't reach their ends.
Inputs may be any that keep to these rules, and one draw needn't show every extreme that they name: `remap_pairs`: tiles of sections 0 to 2 name tiles of section 3, tiles of section 3 name tiles of sections 0 to 2. The 256 entries of one device name tiles of one dom index at most 32 times, and exactly 32 times for some dom index.
All inputs are finite; a program needn't handle non-finite values. No bound on the sum of `land_mask` on one device may be relied on, other than what follows from the above.
Results may differ from the reference program's by a relative error of at most 0.0075.
Values may be sent and summed in bfloat16 or wider, within the bound.
A program may use at most 128 MiB of HBM per device.

```python
import math
import jax
import jax.numpy as jnp
from jax import lax

CELLS = 128
LEVELS = 48
FIELDS = 20
NEIGH = 7
PAIRS = 2
STEPS = 5
TILES = 128
HALO = 32
SECTION_TILES = 1024
CAP = 32
N_COMP = 4
N_DOM = 8


def draw_remap_pairs(key, part):
    key = jax.random.fold_in(key, 11)
    device_count = N_COMP * N_DOM
    entries = TILES * PAIRS
    key_order, key_start, key_tile, key_other = jax.random.split(key, 4)
    order = jax.vmap(lambda sub: jax.random.permutation(sub, entries))(jax.random.split(key_order, device_count))
    start = jax.random.randint(key_start, (device_count, 1), 0, N_DOM)
    column = (start + order // CAP) % N_DOM
    tile_pick = jax.random.randint(key_tile, (device_count, entries), 0, TILES)
    other_side = jax.random.randint(key_other, (device_count, entries), 0, N_COMP - 1)
    source_section = (jnp.arange(device_count, dtype=jnp.int32) // N_DOM)[:, None]
    target_section = jnp.where(source_section < N_COMP - 1, N_COMP - 1, other_side)
    identity = (target_section * N_DOM + column) * TILES + tile_pick
    return identity.reshape(N_COMP, N_DOM * TILES, PAIRS).astype(jnp.int32)


def place_ends(values, own_key, smallest, top_value):
    index_at = [jax.random.randint(jax.random.fold_in(own_key, axis), (), 0, length) for axis, length in enumerate(values.shape)]
    main_axis = values.shape.index(max(values.shape))
    beside = index_at[:main_axis] + [(index_at[main_axis] + 1) % values.shape[main_axis]] + index_at[main_axis + 1:]
    return values.at[tuple(index_at)].set(smallest).at[tuple(beside)].set(top_value)


def block_levels(own_key, dims, shards, smallest, largest):
    level, own = 1.0, jax.random.fold_in(own_key, 6)
    for axis_at, parts in shards:
        steps = jnp.exp(jax.random.uniform(jax.random.fold_in(own, axis_at), (parts,), jnp.float32, smallest / len(shards), largest / len(shards)))
        level = level * jnp.repeat(steps, dims[axis_at] // parts).reshape([-1 if axis == axis_at else 1 for axis in range(len(dims))])
    return level


def centred(key, shape, deviation, most, shards=(), kind=jnp.bfloat16):
    result = jax.random.normal(key, shape, jnp.float32) * deviation
    if len(shards) > 0:
        result = block_levels(key, shape, shards, -0.22, 0.18) * result
    return jnp.clip(result, min=-most, max=most).astype(kind)


def setup_inputs(seed: int = 0) -> dict:
    arg_keys = jax.random.split(jax.random.key(seed), 9)
    model_state = centred(arg_keys[0], (N_COMP, SECTION_TILES, LEVELS, CELLS), 1.0, 6.0, ((0, 4), (1, 8)))
    coefficient = jnp.clip(jnp.exp(math.log(0.5) - 2.306499 * jax.random.uniform(arg_keys[1], (N_COMP, SECTION_TILES, LEVELS, CELLS), jnp.float32) ** block_levels(arg_keys[1], (N_COMP, SECTION_TILES, LEVELS, CELLS), ((0, 4), (1, 8)), -0.2, 0.2)), 0.049804688, 0.5).astype(jnp.bfloat16)
    stencil_blocks = centred(arg_keys[2], (N_COMP, NEIGH, CELLS, CELLS), (CELLS * NEIGH) ** -0.5, 0.1875, ((0, 4),))
    neighbours = place_ends(jax.random.randint(arg_keys[3], (N_COMP, SECTION_TILES, NEIGH), 0, TILES + 2 * HALO), jax.random.fold_in(arg_keys[3], 1), 0, (TILES + 2 * HALO) - 1).astype(jnp.int32)
    land_mask = place_ends((jax.random.randint(arg_keys[4], (SECTION_TILES, CELLS), 0, 4) < 3).astype(jnp.int32), jax.random.fold_in(arg_keys[4], 1), 0, 1)
    surface_flux = centred(arg_keys[5], (N_COMP, SECTION_TILES, FIELDS, CELLS), 1.0, 6.0, ((0, 4), (1, 8)))
    remap_pairs = draw_remap_pairs(jax.random.fold_in(arg_keys[8], 71), 0)
    remap_weights = centred(arg_keys[7], (N_COMP, SECTION_TILES, PAIRS, CELLS, CELLS), CELLS ** -0.5, 0.5, ((0, 4), (1, 8)))
    return {"model_state": model_state, "coefficient": coefficient, "stencil_blocks": stencil_blocks, "neighbours": neighbours, "land_mask": land_mask, "surface_flux": surface_flux, "remap_pairs": remap_pairs, "remap_weights": remap_weights}


def advance_section(current, coefficient, blocks_matrix, neighbours, factor):
    section_rows = current.shape[0]
    row_index = jnp.arange(section_rows, dtype=jnp.int32)
    block_start = (row_index // TILES) * TILES
    source_rows = ((block_start[:, None] + neighbours - HALO) % section_rows).astype(jnp.int32)
    matrix = blocks_matrix.astype(jnp.float32)
    for step_index in range(STEPS):
        def one_block(block_id, present=current):
            first_row = (block_id * TILES).astype(jnp.int32)
            rows_here = lax.dynamic_slice_in_dim(source_rows, first_row, TILES, 0)
            nearby = present[rows_here].astype(jnp.float32)
            summed = jnp.einsum("tklc,kcd->tld", nearby, matrix)
            own_tiles = lax.dynamic_slice_in_dim(present, first_row, TILES, 0).astype(jnp.float32)
            own_coef = lax.dynamic_slice_in_dim(coefficient, first_row, TILES, 0).astype(jnp.float32)
            own_mask = lax.dynamic_slice_in_dim(factor, first_row, TILES, 0)
            return ((own_tiles + own_coef * summed) * own_mask[:, None, :]).astype(jnp.bfloat16)
        current = lax.map(one_block, jnp.arange(N_DOM, dtype=jnp.int32)).reshape(current.shape)
    return current


def section_pieces(fields, weights):
    def one_block(block_id):
        first_row = (block_id * TILES).astype(jnp.int32)
        field_rows = lax.dynamic_slice_in_dim(fields, first_row, TILES, 0).astype(jnp.float32)
        weight_rows = lax.dynamic_slice_in_dim(weights, first_row, TILES, 0).astype(jnp.float32)
        return jnp.einsum("tfc,trcd->trfd", field_rows, weight_rows).astype(jnp.bfloat16)
    pieces = lax.map(one_block, jnp.arange(N_DOM, dtype=jnp.int32))
    return pieces.reshape(SECTION_TILES * PAIRS, FIELDS, CELLS)


def reference(model_state, coefficient, stencil_blocks, neighbours, land_mask, surface_flux, remap_pairs, remap_weights):
    advanced = []
    for section_id in range(N_COMP):
        if section_id == N_COMP - 1:
            factor = land_mask.astype(jnp.float32)
        else:
            factor = jnp.ones(land_mask.shape, jnp.float32)
        advanced.append(advance_section(model_state[section_id], coefficient[section_id], stencil_blocks[section_id], neighbours[section_id], factor))
    next_state = jnp.stack(advanced)
    fields = (surface_flux.astype(jnp.float32) + model_state[:, :, :FIELDS, :].astype(jnp.float32)).astype(jnp.bfloat16)
    total = jnp.zeros((N_COMP * SECTION_TILES, FIELDS, CELLS), jnp.float32)
    for section_id in range(N_COMP):
        pieces = section_pieces(fields[section_id], remap_weights[section_id])
        pieces = lax.optimization_barrier(pieces).astype(jnp.float32)
        targets = remap_pairs[section_id].reshape(SECTION_TILES * PAIRS).astype(jnp.int32)
        section_sum = jax.ops.segment_sum(pieces, targets, num_segments=N_COMP * SECTION_TILES).astype(jnp.bfloat16)
        section_sum = lax.optimization_barrier(section_sum).astype(jnp.float32)
        total = total + section_sum
    remapped = total.reshape(N_COMP, SECTION_TILES, FIELDS, CELLS).astype(jnp.bfloat16)
    return next_state, remapped
```

```python
import functools

import jax
import jax.numpy as jnp
import numpy as np
from jax import lax
from jax.experimental import pallas as pl
from jax.experimental.pallas import tpu as pltpu
from jax.sharding import PartitionSpec as P

STEPS = 5
GROUP = 16
MESH = pl.DeviceIdType.MESH


def coupled_kernel(
    n_dom,
    n_sec,
    cap,
    near_ref,
    entry_ref,
    state_hbm,
    coef_hbm,
    flux_hbm,
    weight_hbm,
    stencil_ref,
    mask_ref,
    code_ref,
    perm_ref,
    next_ref,
    remap_ref,
    buf0,
    buf1,
    buf2,
    buf3,
    buf4,
    coef_ref,
    flux_ref,
    weight_ref,
    lhs_ref,
    out_pieces,
    in_pieces,
    in_codes,
    hit_ref,
    part_ref,
    recv_ref,
    local_sem,
    halo_send,
    halo_recv,
    piece_send,
    piece_recv,
    code_send,
    code_recv,
    part_send,
    part_recv,
):
    bufs = (buf0, buf1, buf2, buf3, buf4)
    tiles, levels, cells = coef_ref.shape
    field_count = flux_ref.shape[1]
    slots_near = near_ref.shape[0] // tiles
    per_tile = weight_ref.shape[0] // tiles
    rim = tiles // 4
    sec = lax.axis_index("comp")
    dom = lax.axis_index("dom")
    last = n_sec - 1
    up = lax.rem(dom + 1, n_dom)
    down = lax.rem(dom + n_dom - 1, n_dom)

    loads = (
        pltpu.make_async_copy(state_hbm, buf0.at[pl.ds(rim, tiles)], local_sem.at[0]),
        pltpu.make_async_copy(flux_hbm, flux_ref, local_sem.at[1]),
        pltpu.make_async_copy(weight_hbm, weight_ref, local_sem.at[2]),
        pltpu.make_async_copy(coef_hbm, coef_ref, local_sem.at[3]),
    )
    for load in loads:
        load.start()

    barrier = pltpu.get_barrier_semaphore()
    for k in range(1, n_dom):
        pl.semaphore_signal(
            barrier, inc=1, device_id=(sec, lax.rem(dom + k, n_dom)), device_id_type=MESH
        )
    for k in range(1, n_sec):
        pl.semaphore_signal(
            barrier, inc=1, device_id=(lax.rem(sec + k, n_sec), dom), device_id_type=MESH
        )
    pl.semaphore_wait(barrier, n_dom - 1 + n_sec - 1)

    def halo(step, side):
        if step == 0:
            source, base = state_hbm, 0
        else:
            source, base = bufs[step], rim
        if side == 0:
            src = source.at[pl.ds(base, rim)]
            dst = bufs[step].at[pl.ds(rim + tiles, rim)]
            target = down
        else:
            src = source.at[pl.ds(base + tiles - rim, rim)]
            dst = bufs[step].at[pl.ds(0, rim)]
            target = up
        return pltpu.make_async_remote_copy(
            src_ref=src,
            dst_ref=dst,
            send_sem=halo_send.at[step, side],
            recv_sem=halo_recv.at[step, side],
            device_id=(sec, target),
            device_id_type=MESH,
        )

    def piece_copy(k):
        target = lax.rem(dom + k, n_dom)
        return pltpu.make_async_remote_copy(
            src_ref=out_pieces.at[k],
            dst_ref=in_pieces.at[dom],
            send_sem=piece_send.at[k],
            recv_sem=piece_recv.at[k],
            device_id=(sec, target),
            device_id_type=MESH,
        )

    def code_copy(k):
        target = lax.rem(dom + k, n_dom)
        return pltpu.make_async_remote_copy(
            src_ref=code_ref.at[target],
            dst_ref=in_codes.at[dom],
            send_sem=code_send.at[k],
            recv_sem=code_recv.at[k],
            device_id=(sec, target),
            device_id_type=MESH,
        )

    for side in range(2):
        halo(0, side).start()
    for k in range(1, n_dom):
        code_copy(k).start()
    in_codes[dom] = code_ref[dom]
    loads[0].wait()
    loads[1].wait()

    def add_surface(block, carry):
        start = block * 8
        own = buf0[pl.ds(rim + start, 8)].astype(jnp.float32)[:, :field_count]
        mixed = flux_ref[pl.ds(start, 8)].astype(jnp.float32) + own
        flux_ref[pl.ds(start, 8)] = mixed.astype(jnp.bfloat16)
        return carry

    lax.fori_loop(0, tiles // 8, add_surface, 0)
    loads[2].wait()

    def make_pieces(target, chunk, store):
        rows = []
        for i in range(16):
            entry = entry_ref[target * cap + chunk * 16 + i]
            rows.append(
                jnp.dot(
                    flux_ref[entry // per_tile],
                    weight_ref[entry],
                    preferred_element_type=jnp.float32,
                )
            )
        stacked = jnp.concatenate(rows, axis=0).astype(jnp.bfloat16)
        sorted_rows = jnp.dot(perm_ref[...], stacked, preferred_element_type=jnp.float32)
        store(chunk, sorted_rows.astype(jnp.bfloat16).reshape(field_count, 16, cells))

    def send_pieces(k, carry):
        target = lax.rem(dom + k, n_dom)

        def store(chunk, value):
            out_pieces[k, :, pl.ds(pl.multiple_of(chunk * 16, 16), 16), :] = value

        def body(chunk, inner):
            make_pieces(target, chunk, store)
            return inner

        lax.fori_loop(0, cap // 16, body, 0)
        piece_copy(k).start()
        return carry

    lax.fori_loop(1, n_dom, send_pieces, 0)

    def own_body(chunk, inner):
        def store(at, value):
            in_pieces[dom, :, pl.ds(pl.multiple_of(at * 16, 16), 16), :] = value

        make_pieces(dom, chunk, store)
        return inner

    lax.fori_loop(0, cap // 16, own_body, 0)
    loads[3].wait()

    def advance(step, first, count):
        source = bufs[step]

        def body(group, carry):
            start = group * GROUP
            for i in range(GROUP):
                for k in range(slots_near):
                    lhs_ref[i * levels : (i + 1) * levels, k * cells : (k + 1) * cells] = source[
                        near_ref[(start + i) * slots_near + k]
                    ]
            summed = jnp.dot(lhs_ref[...], stencil_ref[...], preferred_element_type=jnp.float32)
            summed = summed.reshape(GROUP, levels, cells)
            start = pl.multiple_of(start, GROUP)
            own = source[pl.ds(rim + start, GROUP)].astype(jnp.float32)
            local_coef = coef_ref[pl.ds(start, GROUP)].astype(jnp.float32)
            wet = mask_ref[pl.ds(start, GROUP), :].astype(jnp.float32)
            factor = jnp.where(sec == last, wet, jnp.float32(1.0))
            value = ((own + local_coef * summed) * factor[:, None, :]).astype(jnp.bfloat16)
            if step == STEPS - 1:
                next_ref[pl.ds(start, GROUP)] = value
            else:
                bufs[step + 1][pl.ds(rim + start, GROUP)] = value
            return carry

        lax.fori_loop(first // GROUP, (first + count) // GROUP, body, 0)

    def part_copy(place, slot, target):
        return pltpu.make_async_remote_copy(
            src_ref=part_ref.at[place],
            dst_ref=recv_ref.at[slot],
            send_sem=part_send.at[place],
            recv_sem=part_recv.at[slot],
            device_id=(target, dom),
            device_id_type=MESH,
        )

    def partial_sums(place, target):
        codes = jnp.sum(in_codes[...], axis=0)[0:1, :]
        wanted = target * tiles + lax.broadcasted_iota(jnp.int32, hit_ref.shape, 0)
        hit_ref[...] = (codes == wanted).astype(jnp.float32).astype(jnp.bfloat16)

        def body(field, carry):
            arrived = in_pieces[:, field].reshape(n_dom * cap, cells)
            part_ref[place, field] = jnp.dot(
                hit_ref[...], arrived, preferred_element_type=jnp.float32
            ).astype(jnp.bfloat16)
            return carry

        lax.fori_loop(0, field_count, body, 0)

    def exchange_sections():
        for k in range(1, n_dom):
            piece_copy(k).wait()
            code_copy(k).wait()

        @pl.when(sec != last)
        def _():
            partial_sums(0, last)
            part_copy(0, sec, last).start()

        @pl.when(sec == last)
        def _():
            for target in range(last):
                partial_sums(target, target)
                part_copy(target, 0, target).start()

    for step in range(STEPS):
        for side in range(2):
            halo(step, side).wait()
        if step < STEPS - 1:
            advance(step, 0, rim)
            halo(step + 1, 0).start()
            advance(step, tiles - rim, rim)
            halo(step + 1, 1).start()
            advance(step, rim, tiles - 2 * rim)
        else:
            advance(step, 0, tiles)
        if step == 0:
            exchange_sections()

    @pl.when(sec != last)
    def _():
        part_copy(0, sec, last).wait_send()
        part_copy(0, 0, last).wait_recv()

        def body(field, carry):
            remap_ref[field] = recv_ref[0, field]
            return carry

        lax.fori_loop(0, field_count, body, 0)

    @pl.when(sec == last)
    def _():
        for place in range(last):
            part_copy(place, place, place).wait()

        def body(field, carry):
            total = recv_ref[0, field].astype(jnp.float32)
            for place in range(1, last):
                total = total + recv_ref[place, field].astype(jnp.float32)
            remap_ref[field] = total.astype(jnp.bfloat16)
            return carry

        lax.fori_loop(0, field_count, body, 0)


def slot_tables(pairs, tiles, n_dom, n_sec, cap):
    total = pairs.size
    targets = pairs.reshape(total)
    column = targets // tiles % n_dom
    local_code = targets // (n_dom * tiles) * tiles + targets % tiles
    order = jnp.arange(total, dtype=jnp.int32)
    earlier = (column[:, None] == column[None, :]) & (order[None, :] < order[:, None])
    placed = column * cap + jnp.sum(earlier.astype(jnp.int32), axis=1)
    slot_count = n_dom * cap
    hit = jnp.arange(slot_count, dtype=jnp.int32)[:, None] == placed[None, :]
    packed = order * (2 * n_sec * tiles) + local_code + 1
    found = jnp.sum(jnp.where(hit, packed[None, :], 0), axis=1)
    entry = found // (2 * n_sec * tiles)
    code = found % (2 * n_sec * tiles) - 1
    code = jnp.where(found == 0, n_sec * tiles, code).reshape(n_dom, 1, 1, cap)
    here = (jnp.arange(n_dom, dtype=jnp.int32) == lax.axis_index("dom"))[None, None, :, None]
    rows = jnp.where(here, code, 0).reshape(n_dom, 1, slot_count)
    return entry, jnp.broadcast_to(rows, (n_dom, 8, slot_count))


def local(
    model_state,
    coefficient,
    stencil_blocks,
    neighbours,
    land_mask,
    surface_flux,
    remap_pairs,
    remap_weights,
):
    n_dom = lax.axis_size("dom")
    n_sec = lax.axis_size("comp")
    _, tiles, levels, cells = model_state.shape
    field_count = surface_flux.shape[2]
    near = neighbours.shape[2]
    per_tile = remap_pairs.shape[2]
    total = tiles * per_tile
    cap = max(16, -(-total // n_dom))
    rim = tiles // 4
    entry, codes = slot_tables(remap_pairs[0], tiles, n_dom, n_sec, cap)
    rows = field_count * 16
    at = np.arange(rows)
    perm = np.zeros((rows, rows), np.float32)
    perm[at, (at % 16) * field_count + at // 16] = 1.0
    vmem = pl.BlockSpec(memory_space=pltpu.VMEM)
    smem = pl.BlockSpec(memory_space=pltpu.SMEM)
    anywhere = pl.BlockSpec(memory_space=pl.ANY)
    extended = pltpu.VMEM((tiles + 2 * rim, levels, cells), jnp.bfloat16)
    dma = pltpu.SemaphoreType.DMA
    next_state, remapped = pl.pallas_call(
        functools.partial(coupled_kernel, n_dom, n_sec, cap),
        out_shape=(
            jax.ShapeDtypeStruct((tiles, levels, cells), jnp.bfloat16),
            jax.ShapeDtypeStruct((field_count, tiles, cells), jnp.bfloat16),
        ),
        in_specs=[smem, smem] + [anywhere] * 4 + [vmem] * 4,
        out_specs=(vmem, vmem),
        scratch_shapes=[extended] * STEPS
        + [
            pltpu.VMEM((tiles, levels, cells), jnp.bfloat16),
            pltpu.VMEM((tiles, field_count, cells), jnp.bfloat16),
            pltpu.VMEM((total, cells, cells), jnp.bfloat16),
            pltpu.VMEM((GROUP * levels, near * cells), jnp.bfloat16),
            pltpu.VMEM((n_dom, field_count, cap, cells), jnp.bfloat16),
            pltpu.VMEM((n_dom, field_count, cap, cells), jnp.bfloat16),
            pltpu.VMEM((n_dom, 8, n_dom * cap), jnp.int32),
            pltpu.VMEM((tiles, n_dom * cap), jnp.bfloat16),
            pltpu.VMEM((n_sec - 1, field_count, tiles, cells), jnp.bfloat16),
            pltpu.VMEM((n_sec - 1, field_count, tiles, cells), jnp.bfloat16),
            dma((4,)),
            dma((STEPS, 2)),
            dma((STEPS, 2)),
            dma((n_dom,)),
            dma((n_dom,)),
            dma((n_dom,)),
            dma((n_dom,)),
            dma((n_sec - 1,)),
            dma((n_sec - 1,)),
        ],
        compiler_params=pltpu.CompilerParams(
            collective_id=0, has_side_effects=True, vmem_limit_bytes=56 * 2**20
        ),
    )(
        neighbours.reshape(tiles * near),
        entry,
        model_state[0],
        coefficient[0],
        surface_flux[0],
        remap_weights.reshape(total, cells, cells),
        stencil_blocks.reshape(near * cells, cells),
        land_mask,
        codes,
        jnp.asarray(perm, jnp.bfloat16),
    )
    return (next_state[None], remapped.transpose(1, 0, 2)[None])


def solution(mesh):
    placed = (
        P("comp", "dom", None, None),
        P("comp", "dom", None, None),
        P("comp", None, None, None),
        P("comp", "dom", None),
        P("dom", None),
        P("comp", "dom", None, None),
        P("comp", "dom", None),
        P("comp", "dom", None, None, None),
    )
    return jax.shard_map(
        local,
        mesh=mesh,
        in_specs=placed,
        out_specs=(P("comp", "dom", None, None), P("comp", "dom", None, None)),
        check_vma=False,
    )
```

```python
import functools

import jax
import jax.numpy as jnp
import numpy as np
from jax import lax
from jax.experimental import pallas as pl
from jax.experimental.pallas import tpu as pltpu
from jax.sharding import PartitionSpec as P

STEPS = 5
GROUP = 16
EDGE_PARTS = 2
EARLY = 4
MESH = pl.DeviceIdType.MESH


def coupled_kernel(
    n_dom,
    n_sec,
    cap,
    near_ref,
    entry_ref,
    state_hbm,
    coef_hbm,
    flux_hbm,
    weight_hbm,
    stencil_ref,
    mask_ref,
    code_ref,
    perm_ref,
    next_ref,
    remap_ref,
    buf0,
    buf1,
    buf2,
    buf3,
    buf4,
    coef_ref,
    flux_ref,
    field_ref,
    weight_ref,
    lhs_ref,
    out_pieces,
    in_pieces,
    in_codes,
    hit_ref,
    part_ref,
    recv_ref,
    local_sem,
    halo_send,
    halo_recv,
    piece_send,
    piece_recv,
    code_send,
    code_recv,
    part_send,
    part_recv,
):
    bufs = (buf0, buf1, buf2, buf3, buf4)
    tiles, levels, cells = coef_ref.shape
    field_count = flux_ref.shape[0]
    slots_near = near_ref.shape[0] // tiles
    per_tile = weight_ref.shape[0] // tiles
    rim = tiles // 4
    sec = lax.axis_index("comp")
    dom = lax.axis_index("dom")
    last = n_sec - 1
    up = lax.rem(dom + 1, n_dom)
    down = lax.rem(dom + n_dom - 1, n_dom)

    loads = (
        pltpu.make_async_copy(state_hbm, buf0.at[pl.ds(rim, tiles)], local_sem.at[0]),
        pltpu.make_async_copy(flux_hbm, flux_ref, local_sem.at[1]),
        pltpu.make_async_copy(weight_hbm, weight_ref, local_sem.at[2]),
        pltpu.make_async_copy(coef_hbm, coef_ref, local_sem.at[3]),
    )
    for load in loads:
        load.start()

    barrier = pltpu.get_barrier_semaphore()
    for k in range(1, n_dom):
        pl.semaphore_signal(
            barrier, inc=1, device_id=(sec, lax.rem(dom + k, n_dom)), device_id_type=MESH
        )
    for k in range(1, n_sec):
        pl.semaphore_signal(
            barrier, inc=1, device_id=(lax.rem(sec + k, n_sec), dom), device_id_type=MESH
        )
    pl.semaphore_wait(barrier, n_dom - 1 + n_sec - 1)

    def halo(step, side, part, parts=EDGE_PARTS):
        size = rim // parts
        at = part * size
        if step == 0:
            source, base = state_hbm, 0
        else:
            source, base = bufs[step], rim
        if side == 0:
            src = source.at[pl.ds(base + at, size)]
            dst = bufs[step].at[pl.ds(rim + tiles + at, size)]
            target = down
        else:
            src = source.at[pl.ds(base + tiles - rim + at, size)]
            dst = bufs[step].at[pl.ds(at, size)]
            target = up
        return pltpu.make_async_remote_copy(
            src_ref=src,
            dst_ref=dst,
            send_sem=halo_send.at[step, side * parts + part],
            recv_sem=halo_recv.at[step, side * parts + part],
            device_id=(sec, target),
            device_id_type=MESH,
        )

    def piece_copy(k):
        target = lax.rem(dom + k, n_dom)
        return pltpu.make_async_remote_copy(
            src_ref=out_pieces.at[k],
            dst_ref=in_pieces.at[dom],
            send_sem=piece_send.at[k],
            recv_sem=piece_recv.at[k],
            device_id=(sec, target),
            device_id_type=MESH,
        )

    def code_copy(k):
        target = lax.rem(dom + k, n_dom)
        return pltpu.make_async_remote_copy(
            src_ref=code_ref.at[target],
            dst_ref=in_codes.at[dom],
            send_sem=code_send.at[k],
            recv_sem=code_recv.at[k],
            device_id=(sec, target),
            device_id_type=MESH,
        )

    for part in range(EDGE_PARTS):
        for side in range(2):
            halo(0, side, part).start()
    for k in range(1, n_dom):
        code_copy(k).start()
    in_codes[dom] = code_ref[dom]
    loads[0].wait()
    loads[1].wait()

    def add_surface(block, carry):
        start = pl.multiple_of(block * 16, 16)
        own = buf0[pl.ds(rim + start, 16)].astype(jnp.float32)[:, :field_count]
        by_field = flux_ref[:, pl.ds(start, 16), :].reshape(field_count * 16, cells)
        by_tile = lax.dot_general(
            perm_ref[...],
            by_field,
            (((0,), (0,)), ((), ())),
            preferred_element_type=jnp.float32,
        )
        mixed = by_tile.reshape(16, field_count, cells) + own
        field_ref[pl.ds(start, 16)] = mixed.astype(jnp.bfloat16)
        return carry

    lax.fori_loop(0, tiles // 16, add_surface, 0)
    loads[2].wait()

    def make_pieces(target, chunk, store):
        rows = []
        for i in range(16):
            entry = entry_ref[target * cap + chunk * 16 + i]
            rows.append(
                jnp.dot(
                    field_ref[entry // per_tile],
                    weight_ref[entry],
                    preferred_element_type=jnp.float32,
                )
            )
        stacked = jnp.concatenate(rows, axis=0).astype(jnp.bfloat16)
        sorted_rows = jnp.dot(perm_ref[...], stacked, preferred_element_type=jnp.float32)
        store(chunk, sorted_rows.astype(jnp.bfloat16).reshape(field_count, 16, cells))

    def send_pieces(k, carry):
        target = lax.rem(dom + k, n_dom)

        def store(chunk, value):
            out_pieces[k, :, pl.ds(pl.multiple_of(chunk * 16, 16), 16), :] = value

        def body(chunk, inner):
            make_pieces(target, chunk, store)
            return inner

        lax.fori_loop(0, cap // 16, body, 0)
        piece_copy(k).start()
        return carry

    early = 1 + n_dom * EARLY // 8
    lax.fori_loop(1, early, send_pieces, 0)

    def own_body(chunk, inner):
        def store(at, value):
            in_pieces[dom, :, pl.ds(pl.multiple_of(at * 16, 16), 16), :] = value

        make_pieces(dom, chunk, store)
        return inner

    loads[3].wait()

    def advance(step, first, count):
        source = bufs[step]

        def body(group, carry):
            start = group * GROUP
            for i in range(GROUP):
                for k in range(slots_near):
                    lhs_ref[i * levels : (i + 1) * levels, k * cells : (k + 1) * cells] = source[
                        near_ref[k * tiles + start + i]
                    ]
            summed = jnp.dot(lhs_ref[...], stencil_ref[...], preferred_element_type=jnp.float32)
            summed = summed.reshape(GROUP, levels, cells)
            start = pl.multiple_of(start, GROUP)
            own = source[pl.ds(rim + start, GROUP)].astype(jnp.float32)
            local_coef = coef_ref[pl.ds(start, GROUP)].astype(jnp.float32)
            wet = mask_ref[pl.ds(start, GROUP), :].astype(jnp.float32)
            factor = jnp.where(sec == last, wet, jnp.float32(1.0))
            value = ((own + local_coef * summed) * factor[:, None, :]).astype(jnp.bfloat16)
            if step == STEPS - 1:
                next_ref[pl.ds(start, GROUP)] = value
            else:
                bufs[step + 1][pl.ds(rim + start, GROUP)] = value
            return carry

        lax.fori_loop(first // GROUP, (first + count) // GROUP, body, 0)

    def part_copy(place, slot, target):
        return pltpu.make_async_remote_copy(
            src_ref=part_ref.at[place],
            dst_ref=recv_ref.at[slot],
            send_sem=part_send.at[place],
            recv_sem=part_recv.at[slot],
            device_id=(target, dom),
            device_id_type=MESH,
        )

    def partial_sums(place, target):
        codes = jnp.sum(in_codes[...], axis=0)[0:1, :]
        wanted = target * tiles + lax.broadcasted_iota(jnp.int32, hit_ref.shape, 0)
        hit_ref[...] = (codes == wanted).astype(jnp.float32).astype(jnp.bfloat16)

        def body(field, carry):
            arrived = in_pieces[:, field].reshape(n_dom * cap, cells)
            part_ref[place, field] = jnp.dot(
                hit_ref[...], arrived, preferred_element_type=jnp.float32
            ).astype(jnp.bfloat16)
            return carry

        lax.fori_loop(0, field_count, body, 0)

    def exchange_sections():
        for k in range(1, n_dom):
            piece_copy(k).wait()
            code_copy(k).wait()

        @pl.when(sec != last)
        def _():
            partial_sums(0, last)
            part_copy(0, sec, last).start()

        @pl.when(sec == last)
        def _():
            for target in range(last):
                partial_sums(target, target)
                part_copy(target, 0, target).start()

    for step in range(STEPS):
        for part in range(EDGE_PARTS):
            for side in range(2):
                halo(step, side, part).wait()
        if step < STEPS - 1:
            size = rim // EDGE_PARTS
            for part in range(EDGE_PARTS):
                for side in range(2):
                    advance(step, side * (tiles - rim) + part * size, size)
                    halo(step + 1, side, part).start()
            advance(step, rim, tiles - 2 * rim)
        else:
            advance(step, 0, tiles)
        if step == 0:
            lax.fori_loop(early, n_dom, send_pieces, 0)
            lax.fori_loop(0, cap // 16, own_body, 0)
        if step == 1:
            exchange_sections()

    @pl.when(sec != last)
    def _():
        part_copy(0, sec, last).wait_send()
        part_copy(0, 0, last).wait_recv()

        def body(field, carry):
            remap_ref[field] = recv_ref[0, field]
            return carry

        lax.fori_loop(0, field_count, body, 0)

    @pl.when(sec == last)
    def _():
        for place in range(last):
            part_copy(place, place, place).wait()

        def body(field, carry):
            total = recv_ref[0, field].astype(jnp.float32)
            for place in range(1, last):
                total = total + recv_ref[place, field].astype(jnp.float32)
            remap_ref[field] = total.astype(jnp.bfloat16)
            return carry

        lax.fori_loop(0, field_count, body, 0)


def slot_tables(pairs, tiles, n_dom, n_sec, cap):
    total = pairs.size
    targets = pairs.reshape(total)
    column = targets // tiles % n_dom
    local_code = targets // (n_dom * tiles) * tiles + targets % tiles
    order = jnp.arange(total, dtype=jnp.int32)
    earlier = (column[:, None] == column[None, :]) & (order[None, :] < order[:, None])
    placed = column * cap + jnp.sum(earlier.astype(jnp.int32), axis=1)
    slot_count = n_dom * cap
    hit = jnp.arange(slot_count, dtype=jnp.int32)[:, None] == placed[None, :]
    origin = order % tiles * (total // tiles) + order // tiles
    packed = origin * (2 * n_sec * tiles) + local_code + 1
    found = jnp.sum(jnp.where(hit, packed[None, :], 0), axis=1)
    entry = found // (2 * n_sec * tiles)
    code = found % (2 * n_sec * tiles) - 1
    code = jnp.where(found == 0, n_sec * tiles, code).reshape(n_dom, 1, 1, cap)
    here = (jnp.arange(n_dom, dtype=jnp.int32) == lax.axis_index("dom"))[None, None, :, None]
    rows = jnp.where(here, code, 0).reshape(n_dom, 1, slot_count)
    return entry, jnp.broadcast_to(rows, (n_dom, 8, slot_count))


def local(
    model_state,
    coefficient,
    stencil_blocks,
    neighbours,
    land_mask,
    surface_flux,
    remap_pairs,
    remap_weights,
):
    n_dom = lax.axis_size("dom")
    n_sec = lax.axis_size("comp")
    _, tiles, levels, cells = model_state.shape
    field_count = surface_flux.shape[2]
    near = neighbours.shape[2]
    per_tile = remap_pairs.shape[2]
    total = tiles * per_tile
    cap = max(16, -(-total // n_dom))
    rim = tiles // 4
    entry, codes = slot_tables(remap_pairs[0].T, tiles, n_dom, n_sec, cap)
    rows = field_count * 16
    at = np.arange(rows)
    perm = np.zeros((rows, rows), np.float32)
    perm[at, (at % 16) * field_count + at // 16] = 1.0
    vmem = pl.BlockSpec(memory_space=pltpu.VMEM)
    smem = pl.BlockSpec(memory_space=pltpu.SMEM)
    anywhere = pl.BlockSpec(memory_space=pl.ANY)
    extended = pltpu.VMEM((tiles + 2 * rim, levels, cells), jnp.bfloat16)
    dma = pltpu.SemaphoreType.DMA
    next_state, remapped = pl.pallas_call(
        functools.partial(coupled_kernel, n_dom, n_sec, cap),
        out_shape=(
            jax.ShapeDtypeStruct((tiles, levels, cells), jnp.bfloat16),
            jax.ShapeDtypeStruct((field_count, tiles, cells), jnp.bfloat16),
        ),
        in_specs=[smem, smem] + [anywhere] * 4 + [vmem] * 4,
        out_specs=(vmem, vmem),
        scratch_shapes=[extended] * STEPS
        + [
            pltpu.VMEM((tiles, levels, cells), jnp.bfloat16),
            pltpu.VMEM((field_count, tiles, cells), jnp.bfloat16),
            pltpu.VMEM((tiles, field_count, cells), jnp.bfloat16),
            pltpu.VMEM((total, cells, cells), jnp.bfloat16),
            pltpu.VMEM((GROUP * levels, near * cells), jnp.bfloat16),
            pltpu.VMEM((n_dom, field_count, cap, cells), jnp.bfloat16),
            pltpu.VMEM((n_dom, field_count, cap, cells), jnp.bfloat16),
            pltpu.VMEM((n_dom, 8, n_dom * cap), jnp.int32),
            pltpu.VMEM((tiles, n_dom * cap), jnp.bfloat16),
            pltpu.VMEM((n_sec - 1, field_count, tiles, cells), jnp.bfloat16),
            pltpu.VMEM((n_sec - 1, field_count, tiles, cells), jnp.bfloat16),
            dma((4,)),
            dma((STEPS, 2 * EDGE_PARTS)),
            dma((STEPS, 2 * EDGE_PARTS)),
            dma((n_dom,)),
            dma((n_dom,)),
            dma((n_dom,)),
            dma((n_dom,)),
            dma((n_sec - 1,)),
            dma((n_sec - 1,)),
        ],
        compiler_params=pltpu.CompilerParams(
            collective_id=0, has_side_effects=True, vmem_limit_bytes=56 * 2**20
        ),
    )(
        neighbours[0].T.reshape(near * tiles),
        entry,
        model_state[0],
        coefficient[0],
        surface_flux[0].transpose(1, 0, 2),
        remap_weights.reshape(total, cells, cells),
        stencil_blocks.reshape(near * cells, cells),
        land_mask,
        codes,
        jnp.asarray(perm, jnp.bfloat16),
    )
    return (next_state[None], remapped.transpose(1, 0, 2)[None])


def solution(mesh):
    placed = (
        P("comp", "dom", None, None),
        P("comp", "dom", None, None),
        P("comp", None, None, None),
        P("comp", "dom", None),
        P("dom", None),
        P("comp", "dom", None, None),
        P("comp", "dom", None),
        P("comp", "dom", None, None, None),
    )
    return jax.shard_map(
        local,
        mesh=mesh,
        in_specs=placed,
        out_specs=(P("comp", "dom", None, None), P("comp", "dom", None, None)),
        check_vma=False,
    )
```
